32 devices in a mesh: groups: 2 (over y), expert: 4 (over x, core), tensor: 4 (over z).
Axes of the slice: x: 2, y: 2, z: 4, core: 2. Of those that a mesh axis runs over, the one named last changes fastest.
Arguments:
- tokens: bfloat16 [1536, 3072], P(('groups', 'expert'), 'tensor'), parts along dimension 0, may hold values from -6 to 6
- routes: int32 [1536, 2], P('groups'), parts along dimension 0, may hold values from 0 to 3, all different within a row; in each aligned block of 192 rows (0 to 191, 192 to 383, ...) at most 144 rows name the same one
- probs: float32 [1536, 2], P(('groups', 'expert')), parts along dimension 0, may hold values from 0.2 to 1
- request_adapter: int32 [16], P('groups'), parts along dimension 0, may hold values from 0 to 1
- gate_quant_levels: bfloat16 [4, 3072, 8192], P('expert', None, 'tensor'), may hold values from -127 to 127, as said below
- up_quant_levels: bfloat16 [4, 3072, 8192], P('expert', None, 'tensor'), may hold values from -127 to 127, as said below
- down_quant_levels: bfloat16 [4, 8192, 3072], P('expert', 'tensor'), may hold values from -127 to 127, as said below
- gate_column_scale: float32 [4, 8192], P('expert', 'tensor'), may hold values from 0 to 1, as said below
- up_column_scale: float32 [4, 8192], P('expert', 'tensor'), may hold values from 0 to 1, as said below
- down_column_scale: float32 [4, 3072], P('expert'), may hold values from 0 to 1, as said below
- adapter_input_maps: bfloat16 [4, 3072, 256], P('expert', 'tensor'), may hold values from -0.109375 to 0.109375
- adapter_output_maps: bfloat16 [4, 2, 128, 8192], P('expert', None, None, 'tensor'), may hold values from -0.75 to 0.75
Outputs:
- moe_output: bfloat16 [1536, 3072], P(('groups', 'expert'), 'tensor'), parts along dimension 0
The draws below stay inside these ranges and needn't reach their ends.
There are 2 independent parts, one for each index of `groups`. The reference program is written for one: setup_inputs(seed, part) draws one part's arguments, and reference() takes and returns one part's arrays. A program takes and returns all parts, laid end to end along the dimension named above; an argument that names none is the same for every part. Nothing has to cross between parts.
Inputs may be any that keep to these rules, and one draw needn't show every extreme that they name: `routes`: the two experts of a token differ. In each aligned block of 192 rows (the rows of one index of expert) no expert is named by more than 144 rows, a bound that some block reaches. `gate_quant_levels`: whole numbers. `up_quant_levels`: whole numbers. `down_quant_levels`: whole numbers. `gate_column_scale`: Positive. `up_column_scale`: Positive. `down_column_scale`: Positive.
All inputs are finite; a program needn't handle non-finite values.
Results may differ from the reference program's by a relative error of at most 0.011.
Values may be sent and summed in bfloat16 or wider, within the bound.
A program may use at most 128 MiB of HBM per device.

```python
import math
import jax
import jax.numpy as jnp
import numpy as np
from jax import lax

MODEL_WIDTH = 3072
HIDDEN_UNITS = 8192
ADAPTER_RANK = 64
ADAPTER_COUNT = 2
TOK_DEV = 192
EXPERT_COUNT = 4
CAP = 144
TOKENS = 768
REQS = 8
REQ_LEN = 96
EXPERT_SLOTS = 576
N_TENSOR = 4


def level_matrix(key, shape):
    return jax.random.randint(key, shape, -127, 128).astype(jnp.float32).astype(jnp.bfloat16)


def column_scale(key, shape, fan_in):
    spread_latent = jax.random.uniform(key, shape, jnp.float32, math.log(0.5), math.log(2.0))
    return jnp.exp(spread_latent) / (73.6 * math.sqrt(fan_in))


def draw_gate_quant_levels(key, part):
    key = jax.random.fold_in(key, 11)
    return level_matrix(key, (EXPERT_COUNT, MODEL_WIDTH, HIDDEN_UNITS))


def draw_up_quant_levels(key, part):
    key = jax.random.fold_in(key, 12)
    return level_matrix(key, (EXPERT_COUNT, MODEL_WIDTH, HIDDEN_UNITS))


def draw_down_quant_levels(key, part):
    key = jax.random.fold_in(key, 13)
    return level_matrix(key, (EXPERT_COUNT, HIDDEN_UNITS, MODEL_WIDTH))


def draw_gate_column_scale(key, part):
    key = jax.random.fold_in(key, 14)
    return column_scale(key, (EXPERT_COUNT, HIDDEN_UNITS), MODEL_WIDTH)


def draw_up_column_scale(key, part):
    key = jax.random.fold_in(key, 15)
    return column_scale(key, (EXPERT_COUNT, HIDDEN_UNITS), MODEL_WIDTH)


def draw_down_column_scale(key, part):
    key = jax.random.fold_in(key, 16)
    return column_scale(key, (EXPERT_COUNT, MODEL_WIDTH), HIDDEN_UNITS)


def with_ends(drawn, key, least, top_value):
    shape = drawn.shape
    spot = [jax.random.randint(jax.random.fold_in(key, axis), (), 0, shape[axis]) for axis in range(len(shape))]
    drawn = drawn.at[tuple(spot)].set(least)
    longest = shape.index(max(shape))
    spot[longest] = (spot[longest] + 1) % shape[longest]
    return drawn.at[tuple(spot)].set(top_value)


def steps_of(key, extent, cuts, smallest, top_value):
    gain, own = 1.0, jax.random.fold_in(key, 6)
    for position, blocks in cuts:
        heights = jnp.exp(jax.random.uniform(jax.random.fold_in(own, position), (blocks,), jnp.float32, smallest / len(cuts), top_value / len(cuts)))
        gain = gain * jnp.repeat(heights, extent[position] // blocks).reshape([-1 if axis == position else 1 for axis in range(len(extent))])
    return gain


def assign_block(rng, own, number, rows, count, top, bound, lean):
    ranking = jax.random.permutation(rng, count)
    crowded, common = shares(count, rows * top, bound, lean, True), shares(count, rows * top, bound, lean, False)
    places = jnp.arange(count)

    def named(tallies, turn):
        used = int((tallies > 0).sum())
        fixed = max(1, used // 4)
        moved = fixed + (places - fixed + turn * (used - fixed)) % max(1, count - fixed)
        return jnp.zeros((count,), jnp.int32).at[ranking[jnp.where(places < fixed, places, moved)]].set(jnp.asarray(tallies, jnp.int32))

    tallies = jnp.where(number % 4 == 0, named(crowded, number // 4), named(common, number - number // 4 - 1))
    mixed = jax.random.permutation(jax.random.fold_in(own, 3), count)
    donor, receiver = mixed[0:count // 2 * 2:2], mixed[1:count // 2 * 2:2]
    slack = jnp.minimum(tallies[donor] - 1, bound - tallies[receiver]) // 2
    slack = jnp.where((donor == ranking[0]) | (receiver == ranking[0]) | (tallies[receiver] == 0), 0, jnp.maximum(slack, 0))
    moved = jax.random.randint(jax.random.fold_in(own, 4), (count // 2,), 0, 1 << 20) % (slack + 1)
    tallies = tallies.at[donor].add(-moved).at[receiver].add(moved)
    items = jnp.searchsorted(jnp.cumsum(tallies), jnp.arange(rows * top), side="right").astype(jnp.int32)
    table = items.reshape(top, rows).T
    table = table[jax.random.permutation(jax.random.fold_in(own, 1), rows)]
    turn = jax.random.randint(jax.random.fold_in(own, 2), (rows, 1), 0, top)
    return jnp.take_along_axis(table, (jnp.arange(top)[None, :] + turn) % top, axis=1)


def shares(number_of, total, reach, lean, full):
    weights = [(1 << 20) // math.isqrt(grade ** lean) + 1 for grade in range(1, number_of + 1)]
    largest = reach if full else min(reach, max(-(-total // number_of), total * weights[0] // sum(weights)))
    least = 1 if total - largest >= number_of - 1 else 0
    counts, rest = [largest] + [least] * (number_of - 1), total - largest - least * (number_of - 1)
    while rest > 0:
        free = [i for i in range(1, number_of) if counts[i] < largest] or [i for i in range(1, number_of) if counts[i] < reach]
        pool, budget = sum([weights[i] for i in free]), rest
        for i in free:
            addition = min(reach - counts[i], max(1, budget * weights[i] // pool), rest)
            counts[i] = counts[i] + addition
            rest = rest - addition
    return np.array(counts)


def normal_values(key, dims, width, reach, pieces=(), held_as=jnp.bfloat16):
    result = width * jax.random.normal(key, dims, jnp.float32)
    if pieces:
        result = result * steps_of(key, dims, pieces, -0.22, 0.18)
    return jnp.clip(result, -reach, reach).astype(held_as)


def setup_inputs(seed: int = 0, part: int = 0) -> dict:
    key_of = jax.random.split(jax.random.key(seed), 13)
    own_keys = jax.random.split(jax.random.fold_in(key_of[12], part), 13)
    tokens = normal_values(own_keys[0], (TOKENS, MODEL_WIDTH), 1.0, 6.0, ((0, 4), (1, 4)))
    routes_keys = jax.random.split(jax.random.fold_in(own_keys[1], 1), TOKENS // TOK_DEV)
    routes_turns = jax.random.permutation(jax.random.fold_in(own_keys[1], 3), TOKENS // TOK_DEV)
    routes = jax.vmap(lambda own, number: assign_block(jax.random.fold_in(own_keys[1], 2), own, number, TOK_DEV, EXPERT_COUNT, 2, CAP, 2))(routes_keys, routes_turns).reshape((TOKENS, 2))
    probs = jnp.clip(0.2 + 0.8 * jax.random.uniform(own_keys[2], (TOKENS, 2), jnp.float32) ** steps_of(own_keys[2], (TOKENS, 2), ((0, 4),), -0.2, 0.2), 0.2, 1.0)
    request_adapter = with_ends(jax.random.randint(own_keys[3], (REQS,), 0, ADAPTER_COUNT), jax.random.fold_in(own_keys[3], 1), 0, ADAPTER_COUNT - 1).astype(jnp.int32)
    gate_quant_levels = draw_gate_quant_levels(jax.random.fold_in(key_of[12], 71), part)
    up_quant_levels = draw_up_quant_levels(jax.random.fold_in(key_of[12], 71), part)
    down_quant_levels = draw_down_quant_levels(jax.random.fold_in(key_of[12], 71), part)
    gate_column_scale = draw_gate_column_scale(jax.random.fold_in(key_of[12], 71), part)
    up_column_scale = draw_up_column_scale(jax.random.fold_in(key_of[12], 71), part)
    down_column_scale = draw_down_column_scale(jax.random.fold_in(key_of[12], 71), part)
    adapter_input_maps = normal_values(key_of[10], (EXPERT_COUNT, MODEL_WIDTH, 2 * ADAPTER_COUNT * ADAPTER_RANK), MODEL_WIDTH ** -0.5, 0.109375, ((0, 4), (1, 4)))
    adapter_output_maps = normal_values(key_of[11], (EXPERT_COUNT, 2, ADAPTER_COUNT * ADAPTER_RANK, HIDDEN_UNITS), ADAPTER_RANK ** -0.5, 0.75, ((0, 4), (3, 4)))
    return {"tokens": tokens, "routes": routes, "probs": probs, "request_adapter": request_adapter, "gate_quant_levels": gate_quant_levels, "up_quant_levels": up_quant_levels, "down_quant_levels": down_quant_levels, "gate_column_scale": gate_column_scale, "up_column_scale": up_column_scale, "down_column_scale": down_column_scale, "adapter_input_maps": adapter_input_maps, "adapter_output_maps": adapter_output_maps}


def reference(tokens, routes, probs, request_adapter, gate_quant_levels, up_quant_levels, down_quant_levels, gate_column_scale, up_column_scale, down_column_scale, adapter_input_maps, adapter_output_maps):
    entries = TOKENS * 2
    routes_flat = routes.reshape(entries)
    entry_token = jnp.arange(entries, dtype=jnp.int32) // 2
    entry_adapter = request_adapter[entry_token // REQ_LEN]
    padded_tokens = jnp.concatenate([tokens, jnp.zeros((1, MODEL_WIDTH), tokens.dtype)], axis=0)
    padded_adapter = jnp.concatenate([entry_adapter, jnp.full((1,), -1, jnp.int32)], axis=0)
    hidden_part = HIDDEN_UNITS // N_TENSOR
    adapter_range = jnp.arange(ADAPTER_COUNT, dtype=jnp.int32)

    def one_expert(expert_number):
        picked = jnp.nonzero(routes_flat == expert_number, size=EXPERT_SLOTS, fill_value=entries)[0].astype(jnp.int32)
        incoming_rows = padded_tokens[picked // 2]
        chosen = padded_adapter[picked]
        mask = (chosen[:, None] == adapter_range[None, :]).astype(jnp.float32)
        gate_values = jnp.dot(incoming_rows, gate_quant_levels[expert_number], preferred_element_type=jnp.float32) * gate_column_scale[expert_number]
        upper_values = jnp.dot(incoming_rows, up_quant_levels[expert_number], preferred_element_type=jnp.float32) * up_column_scale[expert_number]
        blended_latent = jnp.dot(incoming_rows, adapter_input_maps[expert_number], preferred_element_type=jnp.float32).reshape(EXPERT_SLOTS, 2, ADAPTER_COUNT, ADAPTER_RANK)
        latent = jnp.sum(blended_latent * mask[:, None, :, None], axis=2).astype(jnp.bfloat16)
        spread_latent = (latent[:, :, None, :] * mask.astype(jnp.bfloat16)[:, None, :, None]).reshape(EXPERT_SLOTS, 2, ADAPTER_COUNT * ADAPTER_RANK)
        gate_values = gate_values + jnp.dot(spread_latent[:, 0], adapter_output_maps[expert_number, 0], preferred_element_type=jnp.float32)
        upper_values = upper_values + jnp.dot(spread_latent[:, 1], adapter_output_maps[expert_number, 1], preferred_element_type=jnp.float32)
        hidden = (jax.nn.silu(gate_values) * upper_values).astype(jnp.bfloat16)
        down_weight = down_quant_levels[expert_number]
        down_gain = down_column_scale[expert_number]

        def add_part(total, index):
            first_unit = index * hidden_part
            segment = lax.dynamic_slice_in_dim(hidden, first_unit, hidden_part, 1)
            weight = lax.dynamic_slice_in_dim(down_weight, first_unit, hidden_part, 0)
            term = (jnp.dot(segment, weight, preferred_element_type=jnp.float32) * down_gain).astype(jnp.bfloat16)
            return total + term.astype(jnp.float32), index

        total = lax.scan(add_part, jnp.zeros((EXPERT_SLOTS, MODEL_WIDTH), jnp.float32), jnp.arange(N_TENSOR, dtype=jnp.int32))[0]
        return total.astype(jnp.bfloat16), picked

    outputs, picks = lax.map(one_expert, jnp.arange(EXPERT_COUNT, dtype=jnp.int32))
    placed = jnp.zeros((entries + 1, MODEL_WIDTH), jnp.bfloat16).at[picks.reshape(-1)].set(outputs.reshape(-1, MODEL_WIDTH))
    per_entry = placed[:entries].astype(jnp.float32).reshape(TOKENS, 2, MODEL_WIDTH)
    return jnp.sum(per_entry * probs[:, :, None], axis=1).astype(jnp.bfloat16)
```

```python
import jax
import jax.numpy as jnp
from jax import lax
from jax.experimental import pallas as pl
from jax.experimental.pallas import tpu as pltpu
from jax.sharding import PartitionSpec as P

ADAPTER_RANK = 64
ADAPTER_COUNT = 2


def slot_positions(routes_flat, expert_count):
    experts_range = jnp.arange(expert_count, dtype=jnp.int32)
    onehot = (routes_flat[..., None] == experts_range).astype(jnp.int32)
    earlier = jnp.cumsum(onehot, axis=1) - onehot
    return jnp.sum(onehot * earlier, axis=-1)


def slot_sources(routes_flat, positions, expert_count, capacity, tok_dev):
    blocks = routes_flat.shape[0]
    entries = routes_flat.shape[1]
    experts_range = jnp.arange(expert_count, dtype=jnp.int32)
    slot_range = jnp.arange(capacity, dtype=jnp.int32)
    matched = (
        (routes_flat[None, :, None, :] == experts_range[:, None, None, None])
        & (positions[None, :, None, :] == slot_range[None, None, :, None])
    ).astype(jnp.int32)
    source_row = (
        jnp.arange(blocks, dtype=jnp.int32)[:, None] * tok_dev
        + jnp.arange(entries, dtype=jnp.int32)[None, :] // 2
    )
    found = jnp.sum(matched, axis=-1)
    return jnp.sum(matched * source_row[None, :, None, :], axis=-1) + (1 - found) * (
        blocks * tok_dev
    )


def slot_adapters(routes_flat, positions, entry_adapter, expert_index, capacity):
    slot_range = jnp.arange(capacity, dtype=jnp.int32)
    matched = (
        (routes_flat == expert_index)[:, None, :]
        & (positions[:, None, :] == slot_range[None, :, None])
    ).astype(jnp.float32)
    adapter_hot = (entry_adapter[..., None] == jnp.arange(ADAPTER_COUNT, dtype=jnp.int32)).astype(
        jnp.float32
    )
    return jnp.einsum("bsj,bja->bsa", matched, adapter_hot)


def body(
    tokens,
    routes,
    probs,
    request_adapter,
    gate_quant_levels,
    up_quant_levels,
    down_quant_levels,
    gate_column_scale,
    up_column_scale,
    down_column_scale,
    adapter_input_maps,
    adapter_output_maps,
):
    expert_count = lax.axis_size("expert")
    expert_index = lax.axis_index("expert")
    tok_dev = tokens.shape[0]
    width_part = tokens.shape[1]
    capacity = max(2, min(tok_dev, 3 * (2 * tok_dev // expert_count) // 2))
    slot_count = expert_count * capacity
    requests = request_adapter.shape[0]
    request_length = routes.shape[0] // requests
    routes_flat = routes.reshape(expert_count, 2 * tok_dev)
    positions = slot_positions(routes_flat, expert_count)
    entry_token = (
        jnp.arange(expert_count, dtype=jnp.int32)[:, None] * tok_dev
        + jnp.arange(2 * tok_dev, dtype=jnp.int32)[None, :] // 2
    )
    entry_request = entry_token // request_length
    request_hot = (entry_request[..., None] == jnp.arange(requests, dtype=jnp.int32)).astype(
        jnp.int32
    )
    entry_adapter = jnp.sum(request_hot * request_adapter, axis=-1)
    table = slot_adapters(routes_flat, positions, entry_adapter, expert_index, capacity).reshape(
        -1, ADAPTER_COUNT
    )
    own_routes = lax.dynamic_slice_in_dim(routes_flat, expert_index, 1, 0)[0]
    own_positions = lax.dynamic_slice_in_dim(positions, expert_index, 1, 0)[0]
    sources = slot_sources(
        own_routes[None], own_positions[None], expert_count, capacity, tok_dev
    ).reshape(-1)
    gate_weight = gate_quant_levels[0]
    up_weight = up_quant_levels[0]
    adapter_row_block = adapter_input_maps[0]
    padded = jnp.concatenate([tokens, jnp.zeros((1, width_part), jnp.bfloat16)], axis=0)
    outgoing = jnp.take(padded, sources, axis=0).reshape(expert_count, capacity, width_part)
    arrived = lax.all_to_all(outgoing, "expert", split_axis=0, concat_axis=0, tiled=True).reshape(
        -1, width_part
    )
    piece = lax.all_gather(arrived, "tensor", axis=1, tiled=True)
    gate_next = jnp.dot(piece, gate_weight, preferred_element_type=jnp.float32)
    up_next = jnp.dot(piece, up_weight, preferred_element_type=jnp.float32)
    mixed = jnp.dot(arrived, adapter_row_block, preferred_element_type=jnp.float32)
    gate_plain_term = gate_next * gate_column_scale[0]
    up_plain_term = up_next * up_column_scale[0]
    selected = jnp.sum(
        mixed.reshape(-1, 2, ADAPTER_COUNT, ADAPTER_RANK) * table[:, None, :, None], axis=2
    ).reshape(-1, 2 * ADAPTER_RANK)
    selected = lax.psum(selected, "tensor")
    latent = selected.astype(jnp.bfloat16).reshape(-1, 2, ADAPTER_RANK)
    spread_latent = (latent[:, :, None, :] * table.astype(jnp.bfloat16)[:, None, :, None]).reshape(
        -1, 2, ADAPTER_COUNT * ADAPTER_RANK
    )
    gate_values = gate_plain_term + jnp.dot(
        spread_latent[:, 0], adapter_output_maps[0, 0], preferred_element_type=jnp.float32
    )
    upper_values = up_plain_term + jnp.dot(
        spread_latent[:, 1], adapter_output_maps[0, 1], preferred_element_type=jnp.float32
    )
    hidden = (jax.nn.silu(gate_values) * upper_values).astype(jnp.bfloat16)
    down_weight = down_quant_levels[0]
    down_gain = down_column_scale[0]
    term = lax.dot_general(
        down_weight, hidden, (((0,), (1,)), ((), ())), preferred_element_type=jnp.float32
    )
    summed = lax.psum_scatter(
        (term * down_gain[:, None]).astype(jnp.bfloat16), "tensor", scatter_dimension=0, tiled=True
    )
    returned = lax.all_to_all(
        summed.reshape(width_part, expert_count, capacity),
        "expert",
        split_axis=1,
        concat_axis=1,
        tiled=True,
    ).reshape(width_part, slot_count)
    targets = own_routes * capacity + own_positions
    match = (
        (jnp.arange(slot_count, dtype=jnp.int32)[:, None] == targets[None, :])
        .astype(jnp.float32)
        .reshape(slot_count, tok_dev, 2)
    )
    combine = jnp.sum(match * probs[None, :, :], axis=2)
    output = lax.dot_general(
        combine,
        returned.astype(jnp.float32),
        (((0,), (1,)), ((), ())),
        precision=lax.Precision.HIGHEST,
        preferred_element_type=jnp.float32,
    )
    return output.astype(jnp.bfloat16)


MESH_ID = pl.DeviceIdType.MESH


def rcopy(src, dst, send, recv, device):
    return pltpu.make_async_remote_copy(
        src_ref=src, dst_ref=dst, send_sem=send, recv_sem=recv, device_id=device, device_id_type=MESH_ID
    )


def layer_kernel(
    tok, meta, pt, ain, aout, gs, us, ds, wg, wu, wd, out,
    X, wbuf, wdb, acc, hid, lat_s, lat_r, spread, pbuf, wrow, part, rs_buf, rx_buf, rz_buf,
    local_sem, w_sem, wd_sem, x_recv, z_send, x_send, sib_send, fwd_send,
    p_send, p_recv, lat_send, lat_recv, ps_send, ps_recv, px_send, px_recv, pz_send, pz_recv,
):
    rows, width = tok.shape
    hidden = wbuf.shape[3]
    all_rows = 4 * rows
    g, e, z = lax.axis_index("groups"), lax.axis_index("expert"), lax.axis_index("tensor")
    core = e % 2
    e1 = e + 1 - 2 * core
    e2 = (e + 2) % 4
    e3 = (e1 + 2) % 4
    pair_x, pair_own = 1 - e // 2, e // 2
    h = z // 2
    zz = z * (1 - h) + (3 - z) * h
    order = [b * (1 - h) + (3 - b) * h for b in (zz, 1 - zz, 2, 3)]
    inner = z + 1 - 2 * h
    outer = (z - 1 + 2 * h + 4) % 4
    others_e = (e1, e2, e3)
    others_z = tuple((z + d) % 4 for d in (1, 2, 3))

    def wload(k):
        s, slot = order[k], k % 2
        at = pl.ds(pl.multiple_of(s * width, width), width)
        return [
            pltpu.make_async_copy(w.at[at, :], wbuf.at[slot, i], w_sem.at[slot, i])
            for i, w in enumerate((wg, wu))
        ]

    def wdload(i):
        s = order[3 - i]
        return pltpu.make_async_copy(
            wd.at[:, pl.ds(pl.multiple_of(s * width, width), width)], wdb.at[i], wd_sem.at[i]
        )

    for k in (0, 1):
        for c in wload(k):
            c.start()
    barrier = pltpu.get_barrier_semaphore()
    for o in others_e:
        pl.semaphore_signal(barrier, inc=1, device_id=(g, o, z), device_id_type=MESH_ID)
    for o in others_z:
        pl.semaphore_signal(barrier, inc=1, device_id=(g, e, o), device_id_type=MESH_ID)
    pl.semaphore_wait(barrier, 6)

    def to_z(k, target, send_index, src=None):
        s = order[k]
        return rcopy(X.at[s, e] if src is None else src, X.at[s, e], z_send.at[send_index], x_recv.at[s, e], (g, e, target))

    def to_x(k, src=None):
        s = order[k]
        return rcopy(X.at[s, e] if src is None else src, X.at[s, e], x_send.at[k], x_recv.at[s, e], (g, e2, z))

    def to_sib(k, src=None):
        s = order[k]
        return rcopy(X.at[s, e] if src is None else src, X.at[s, e], sib_send.at[k], x_recv.at[s, e], (g, e1, z))

    def fwd_sib(k):
        s = order[k]
        return rcopy(X.at[s, e2], X.at[s, e2], fwd_send.at[k], x_recv.at[s, e2], (g, e1, z))

    def arrived(k, b):
        s = order[k]
        rcopy(X.at[s, b], X.at[s, b], x_send.at[k], x_recv.at[s, b], (g, e2, z)).wait_recv()

    p_copies = [rcopy(pt, pbuf.at[e], p_send.at[i], p_recv.at[e], (g, o, z)) for i, o in enumerate(others_e)]

    to_x(0, tok).start()
    to_z(0, inner, 0, tok).start()

    @pl.when(zz == 1)
    def _():
        to_z(0, outer, 4, tok).start()

    to_sib(0, tok).start()
    for c in p_copies:
        c.start()
    for i in range(4):
        wdload(i).start()
    own = pltpu.make_async_copy(tok, X.at[z, e], local_sem)
    own.start()
    own.wait()

    def forward(k):
        arrived(k, e)

        @pl.when(zz == 1)
        def _():
            to_z(k, inner if k == 1 else outer, k).start()

        to_x(k).start()
        to_sib(k).start()

    lane = lax.broadcasted_iota(jnp.int32, (all_rows, 128), 1)
    lat_copies = [
        rcopy(lat_s, lat_r.at[z], lat_send.at[i], lat_recv.at[z], (g, e, o)) for i, o in enumerate(others_z)
    ]

    for k in range(4):
        s, slot = order[k], k % 2
        if k == 0:
            forward(1)
        if k < 2:
            @pl.when(zz == 1)
            def _():
                forward(k + 2)

            @pl.when(zz == 0)
            def _():
                if k > 0:
                    forward(k + 1)
        if k == 2:
            @pl.when(zz == 0)
            def _():
                forward(3)
        arrived(k, e2)
        fwd_sib(k).start()
        arrived(k, e1)
        arrived(k, e3)
        if k == 0:
            a = meta[:, 2:3]
            keep = jnp.where(lane < 64, 1.0 - a, a)
            mixed = jnp.dot(X[s].reshape(all_rows, width), ain[...], preferred_element_type=jnp.float32)
            m0, m1 = mixed[:, :128] * keep, mixed[:, 128:] * keep
            m0 = m0 + pltpu.roll(m0, 64, 1)
            m1 = m1 + pltpu.roll(m1, 64, 1)
            lat_s[...] = jnp.where(lane < 64, m0, m1).astype(jnp.bfloat16)
            for c in lat_copies:
                c.start()
            pbuf[e] = pt[...]
        if k == 2:
            for o in others_e:
                rcopy(pt, pbuf.at[o], p_send.at[0], p_recv.at[o], (g, e2, z)).wait_recv()
            for b in range(4):
                p = pbuf[b].T
                m = meta[b * rows:(b + 1) * rows, :]
                w = p[:rows, 0:1] * m[:, 0:1] + p[:rows, 1:2] * m[:, 1:2]
                wrow[b // 2, (b % 2) * rows:(b % 2 + 1) * rows, :] = jnp.broadcast_to(w, (rows, 128))
        if k == 3:
            for o in others_z:
                rcopy(lat_s, lat_r.at[o], lat_send.at[0], lat_recv.at[o], (g, e, inner)).wait_recv()
            total = lat_s[...].astype(jnp.float32)
            for o in others_z:
                total = total + lat_r[o].astype(jnp.float32)
            a = meta[:, 2:3]
            keep = jnp.where(lane < 64, 1.0 - a, a)
            turned = pltpu.roll(total, 64, 1)
            spread[0] = (jnp.where(lane < 64, total, turned) * keep).astype(jnp.bfloat16)
            spread[1] = (jnp.where(lane < 64, turned, total) * keep).astype(jnp.bfloat16)
        for c in wload(k):
            c.wait()

        if k < 3:
            @pl.loop(0, hidden // 256)
            def _(j):
                at = pl.ds(pl.multiple_of(j * 256, 256), 256)
                for i in range(2):
                    d = jnp.dot(
                        X[s].reshape(all_rows, width), wbuf[slot, i, :, at], preferred_element_type=jnp.float32
                    )
                    if k == 0:
                        acc[i, :, at] = d
                    else:
                        acc[i, :, at] += d
        else:
            @pl.loop(0, hidden // 256)
            def _(j):
                at = pl.ds(pl.multiple_of(j * 256, 256), 256)
                x = X[s].reshape(all_rows, width)
                v = acc[0, :, at] + jnp.dot(x, wbuf[slot, 0, :, at], preferred_element_type=jnp.float32)
                u = acc[1, :, at] + jnp.dot(x, wbuf[slot, 1, :, at], preferred_element_type=jnp.float32)
                v = v * gs[:, at] + jnp.dot(spread[0], aout[0, :, at], preferred_element_type=jnp.float32)
                u = u * us[:, at] + jnp.dot(spread[1], aout[1, :, at], preferred_element_type=jnp.float32)
                y = (v / (1.0 + jnp.exp(-v)) * u).astype(jnp.bfloat16)
                hid[:, :, at] = y.reshape(2, 2 * rows, 256)
        if k < 2:
            for c in wload(k + 2):
                c.start()

    def s_copy(n, i):
        return rcopy(part.at[n, i, 1 - core], rs_buf.at[n, i], ps_send.at[n, i], ps_recv.at[n, i], (g, e1, z))

    def x_copy(i):
        return rcopy(part.at[0, i, core], rx_buf.at[i], px_send.at[i], px_recv.at[i], (g, e2, z))

    def z_copy(i):
        return rcopy(part.at[1, i, core], rz_buf.at[z], pz_send.at[i], pz_recv.at[z], (g, e, order[3 - i]))

    def down(n, i):
        pair = (pair_x, pair_own)[n]
        s = order[3 - i]
        if n == 0:
            wdload(i).wait()

        @pl.loop(0, width // 256)
        def _(j):
            at = pl.ds(pl.multiple_of(j * 256, 256), 256)
            d = jnp.dot(hid[pair], wdb[i, :, at], preferred_element_type=jnp.float32)
            d = d * ds[pl.ds(s, 1), at] * wrow[pair, :, 0:1]
            part[n, i, :, :, at] = d.astype(jnp.bfloat16).reshape(2, rows, 256)
        s_copy(n, i).start()

    def send_x(i):
        s_copy(0, i).wait_recv()
        part[0, i, core] = (part[0, i, core].astype(jnp.float32) + rs_buf[0, i].astype(jnp.float32)).astype(
            jnp.bfloat16
        )
        x_copy(i).start()

    def gathered(i):
        s_copy(1, i).wait_recv()
        x_copy(i).wait_recv()
        return (
            part[1, i, core].astype(jnp.float32)
            + rs_buf[1, i].astype(jnp.float32)
            + rx_buf[i].astype(jnp.float32)
        )

    for i in range(4):
        down(0, i)
        if i > 0:
            send_x(i - 1)
    for i in range(4):
        down(1, i)
        if i == 0:
            send_x(3)
    for i in range(3):
        part[1, i, core] = gathered(i).astype(jnp.bfloat16)
        z_copy(i).start()
    total = gathered(3)
    for o in others_z:
        rcopy(rz_buf.at[o], rz_buf.at[o], pz_send.at[0], pz_recv.at[o], (g, e, inner)).wait_recv()
        total = total + rz_buf[o].astype(jnp.float32)
    out[...] = total.astype(jnp.bfloat16)

    to_z(0, inner, 0, tok).wait_send()

    @pl.when(zz == 1)
    def _():
        to_z(0, outer, 4, tok).wait_send()
        for k in (1, 2, 3):
            to_z(k, inner if k == 1 else outer, k).wait_send()

    for k in range(4):
        to_x(k).wait_send()
        to_sib(k).wait_send()
        fwd_sib(k).wait_send()
        x_copy(k).wait_send()
        for n in range(2):
            s_copy(n, k).wait_send()
    for c in p_copies + lat_copies:
        c.wait_send()
    for i in range(3):
        z_copy(i).wait_send()


def fused_body(
    tokens, routes, probs, request_adapter, gate_quant_levels, up_quant_levels, down_quant_levels,
    gate_column_scale, up_column_scale, down_column_scale, adapter_input_maps, adapter_output_maps,
):
    rows, width = tokens.shape
    hidden = gate_quant_levels.shape[2]
    all_rows = routes.shape[0]
    e = lax.axis_index("expert")
    per = all_rows // request_adapter.shape[0]
    adapter = jnp.broadcast_to(request_adapter[:, None], (request_adapter.shape[0], per)).reshape(-1, 1)
    meta = jnp.concatenate(
        [(routes == e).astype(jnp.float32), adapter.astype(jnp.float32), jnp.zeros((all_rows, 125), jnp.float32)],
        axis=1,
    )
    pt = jnp.pad(probs.T, ((0, 6), (0, 256 - rows)))
    ds = down_column_scale.reshape(4, width)
    vm = pl.BlockSpec(memory_space=pltpu.VMEM)
    hbm = pl.BlockSpec(memory_space=pl.ANY)
    bf, f32 = jnp.bfloat16, jnp.float32
    dma = pltpu.SemaphoreType.DMA
    return pl.pallas_call(
        layer_kernel,
        out_shape=jax.ShapeDtypeStruct((rows, width), bf),
        in_specs=[vm] * 8 + [hbm] * 3,
        out_specs=vm,
        scratch_shapes=[
            pltpu.VMEM((4, 4, rows, width), bf),
            pltpu.VMEM((2, 2, width, hidden), bf),
            pltpu.VMEM((4, hidden, width), bf),
            pltpu.VMEM((2, all_rows, hidden), f32),
            pltpu.VMEM((2, 2 * rows, hidden), bf),
            pltpu.VMEM((all_rows, 128), bf),
            pltpu.VMEM((4, all_rows, 128), bf),
            pltpu.VMEM((2, all_rows, 128), bf),
            pltpu.VMEM((4, 8, 256), f32),
            pltpu.VMEM((2, 2 * rows, 128), f32),
            pltpu.VMEM((2, 4, 2, rows, width), bf),
            pltpu.VMEM((2, 4, rows, width), bf),
            pltpu.VMEM((4, rows, width), bf),
            pltpu.VMEM((4, rows, width), bf),
            dma, dma((2, 2)), dma((4,)), dma((4, 4)), dma((5,)), dma((4,)), dma((4,)), dma((4,)),
            dma((3,)), dma((4,)), dma((3,)), dma((4,)), dma((2, 4)), dma((2, 4)), dma((4,)), dma((4,)),
            dma((3,)), dma((4,)),
        ],
        compiler_params=pltpu.CompilerParams(
            collective_id=0, has_side_effects=True, vmem_limit_bytes=63 * 1024 * 1024
        ),
        cost_estimate=pl.CostEstimate(
            flops=6 * all_rows * 4 * width * hidden, bytes_accessed=6 * 4 * width * hidden, transcendentals=0
        ),
        name="moe_layer",
    )(
        tokens, meta, pt, adapter_input_maps[0], adapter_output_maps[0], gate_column_scale, up_column_scale, ds,
        gate_quant_levels[0], up_quant_levels[0], down_quant_levels[0],
    )


def solution(mesh):
    small = mesh.shape["expert"] == 4 and mesh.shape["tensor"] == 4
    return jax.shard_map(
        fused_body if small else body,
        mesh=mesh,
        in_specs=(
            P(("groups", "expert"), "tensor"),
            P("groups", None),
            P(("groups", "expert"), None),
            P("groups"),
            P("expert", None, "tensor"),
            P("expert", None, "tensor"),
            P("expert", "tensor", None),
            P("expert", "tensor"),
            P("expert", "tensor"),
            P("expert", None),
            P("expert", "tensor", None),
            P("expert", None, None, "tensor"),
        ),
        out_specs=P(("groups", "expert"), "tensor"),
        check_vma=False,
    )
```

```python
import jax
import jax.numpy as jnp
from jax import lax
from jax.experimental import pallas as pl
from jax.experimental.pallas import tpu as pltpu
from jax.sharding import PartitionSpec as P

ADAPTER_RANK = 64
ADAPTER_COUNT = 2


def slot_positions(routes_flat, expert_count):
    experts_range = jnp.arange(expert_count, dtype=jnp.int32)
    onehot = (routes_flat[..., None] == experts_range).astype(jnp.int32)
    earlier = jnp.cumsum(onehot, axis=1) - onehot
    return jnp.sum(onehot * earlier, axis=-1)


def slot_sources(routes_flat, positions, expert_count, capacity, tok_dev):
    blocks = routes_flat.shape[0]
    entries = routes_flat.shape[1]
    experts_range = jnp.arange(expert_count, dtype=jnp.int32)
    slot_range = jnp.arange(capacity, dtype=jnp.int32)
    matched = (
        (routes_flat[None, :, None, :] == experts_range[:, None, None, None])
        & (positions[None, :, None, :] == slot_range[None, None, :, None])
    ).astype(jnp.int32)
    source_row = (
        jnp.arange(blocks, dtype=jnp.int32)[:, None] * tok_dev
        + jnp.arange(entries, dtype=jnp.int32)[None, :] // 2
    )
    found = jnp.sum(matched, axis=-1)
    return jnp.sum(matched * source_row[None, :, None, :], axis=-1) + (1 - found) * (
        blocks * tok_dev
    )


def slot_adapters(routes_flat, positions, entry_adapter, expert_index, capacity):
    slot_range = jnp.arange(capacity, dtype=jnp.int32)
    matched = (
        (routes_flat == expert_index)[:, None, :]
        & (positions[:, None, :] == slot_range[None, :, None])
    ).astype(jnp.float32)
    adapter_hot = (entry_adapter[..., None] == jnp.arange(ADAPTER_COUNT, dtype=jnp.int32)).astype(
        jnp.float32
    )
    return jnp.einsum("bsj,bja->bsa", matched, adapter_hot)


def body(
    tokens,
    routes,
    probs,
    request_adapter,
    gate_quant_levels,
    up_quant_levels,
    down_quant_levels,
    gate_column_scale,
    up_column_scale,
    down_column_scale,
    adapter_input_maps,
    adapter_output_maps,
):
    expert_count = lax.axis_size("expert")
    expert_index = lax.axis_index("expert")
    tok_dev = tokens.shape[0]
    width_part = tokens.shape[1]
    capacity = max(2, min(tok_dev, 3 * (2 * tok_dev // expert_count) // 2))
    slot_count = expert_count * capacity
    requests = request_adapter.shape[0]
    request_length = routes.shape[0] // requests
    routes_flat = routes.reshape(expert_count, 2 * tok_dev)
    positions = slot_positions(routes_flat, expert_count)
    entry_token = (
        jnp.arange(expert_count, dtype=jnp.int32)[:, None] * tok_dev
        + jnp.arange(2 * tok_dev, dtype=jnp.int32)[None, :] // 2
    )
    entry_request = entry_token // request_length
    request_hot = (entry_request[..., None] == jnp.arange(requests, dtype=jnp.int32)).astype(
        jnp.int32
    )
    entry_adapter = jnp.sum(request_hot * request_adapter, axis=-1)
    table = slot_adapters(routes_flat, positions, entry_adapter, expert_index, capacity).reshape(
        -1, ADAPTER_COUNT
    )
    own_routes = lax.dynamic_slice_in_dim(routes_flat, expert_index, 1, 0)[0]
    own_positions = lax.dynamic_slice_in_dim(positions, expert_index, 1, 0)[0]
    sources = slot_sources(
        own_routes[None], own_positions[None], expert_count, capacity, tok_dev
    ).reshape(-1)
    gate_weight = gate_quant_levels[0]
    up_weight = up_quant_levels[0]
    adapter_row_block = adapter_input_maps[0]
    padded = jnp.concatenate([tokens, jnp.zeros((1, width_part), jnp.bfloat16)], axis=0)
    outgoing = jnp.take(padded, sources, axis=0).reshape(expert_count, capacity, width_part)
    arrived = lax.all_to_all(outgoing, "expert", split_axis=0, concat_axis=0, tiled=True).reshape(
        -1, width_part
    )
    piece = lax.all_gather(arrived, "tensor", axis=1, tiled=True)
    gate_next = jnp.dot(piece, gate_weight, preferred_element_type=jnp.float32)
    up_next = jnp.dot(piece, up_weight, preferred_element_type=jnp.float32)
    mixed = jnp.dot(arrived, adapter_row_block, preferred_element_type=jnp.float32)
    gate_plain_term = gate_next * gate_column_scale[0]
    up_plain_term = up_next * up_column_scale[0]
    selected = jnp.sum(
        mixed.reshape(-1, 2, ADAPTER_COUNT, ADAPTER_RANK) * table[:, None, :, None], axis=2
    ).reshape(-1, 2 * ADAPTER_RANK)
    selected = lax.psum(selected, "tensor")
    latent = selected.astype(jnp.bfloat16).reshape(-1, 2, ADAPTER_RANK)
    spread_latent = (latent[:, :, None, :] * table.astype(jnp.bfloat16)[:, None, :, None]).reshape(
        -1, 2, ADAPTER_COUNT * ADAPTER_RANK
    )
    gate_values = gate_plain_term + jnp.dot(
        spread_latent[:, 0], adapter_output_maps[0, 0], preferred_element_type=jnp.float32
    )
    upper_values = up_plain_term + jnp.dot(
        spread_latent[:, 1], adapter_output_maps[0, 1], preferred_element_type=jnp.float32
    )
    hidden = (jax.nn.silu(gate_values) * upper_values).astype(jnp.bfloat16)
    down_weight = down_quant_levels[0]
    down_gain = down_column_scale[0]
    term = lax.dot_general(
        down_weight, hidden, (((0,), (1,)), ((), ())), preferred_element_type=jnp.float32
    )
    summed = lax.psum_scatter(
        (term * down_gain[:, None]).astype(jnp.bfloat16), "tensor", scatter_dimension=0, tiled=True
    )
    returned = lax.all_to_all(
        summed.reshape(width_part, expert_count, capacity),
        "expert",
        split_axis=1,
        concat_axis=1,
        tiled=True,
    ).reshape(width_part, slot_count)
    targets = own_routes * capacity + own_positions
    match = (
        (jnp.arange(slot_count, dtype=jnp.int32)[:, None] == targets[None, :])
        .astype(jnp.float32)
        .reshape(slot_count, tok_dev, 2)
    )
    combine = jnp.sum(match * probs[None, :, :], axis=2)
    output = lax.dot_general(
        combine,
        returned.astype(jnp.float32),
        (((0,), (1,)), ((), ())),
        precision=lax.Precision.HIGHEST,
        preferred_element_type=jnp.float32,
    )
    return output.astype(jnp.bfloat16)


MESH_ID = pl.DeviceIdType.MESH


def rcopy(src, dst, send, recv, device):
    return pltpu.make_async_remote_copy(
        src_ref=src, dst_ref=dst, send_sem=send, recv_sem=recv, device_id=device, device_id_type=MESH_ID
    )


def layer_kernel(
    req, tok, routes, probs, ain, aout, gs, us, ds, wg, wu, wd, out,
    X, wbuf, wdb, acc, hid, lat_s, lat_r, lat_t, spread, keep_s, turn_s, pt, pbuf, wrow, part, rs_buf, rx_buf, rz_buf,
    local_sem, w_sem, wd_sem, x_recv, z_send, x_send, sib_send, fwd_send,
    p_send, p_recv, lat_send, lat_recv, lt_send, lt_recv, ps_send, ps_recv, px_send, px_recv, pz_send, pz_recv,
):
    rows, width = tok.shape
    hidden = wbuf.shape[3]
    all_rows = 4 * rows
    g, e, z = lax.axis_index("groups"), lax.axis_index("expert"), lax.axis_index("tensor")
    core = e % 2
    e1 = e + 1 - 2 * core
    e2 = (e + 2) % 4
    e3 = (e1 + 2) % 4
    pair_x, pair_own = 1 - e // 2, e // 2
    h = z // 2
    zz = z * (1 - h) + (3 - z) * h
    order = [b * (1 - h) + (3 - b) * h for b in (zz, 1 - zz, 2, 3)]
    inner = z + 1 - 2 * h
    outer = (z - 1 + 2 * h + 4) % 4
    others_e = (e1, e2, e3)
    others_z = tuple((z + d) % 4 for d in (1, 2, 3))

    def wload(k):
        s, slot = order[k], k % 2
        at = pl.ds(pl.multiple_of(s * width, width), width)
        return [
            pltpu.make_async_copy(w.at[at, :], wbuf.at[slot, i], w_sem.at[slot, i])
            for i, w in enumerate((wg, wu))
        ]

    def wdload(i):
        s = order[3 - i]
        return pltpu.make_async_copy(
            wd.at[:, pl.ds(pl.multiple_of(s * width, width), width)], wdb.at[i], wd_sem.at[i]
        )

    for k in (0, 1):
        for c in wload(k):
            c.start()
    barrier = pltpu.get_barrier_semaphore()
    for o in others_e:
        pl.semaphore_signal(barrier, inc=1, device_id=(g, o, z), device_id_type=MESH_ID)
    for o in others_z:
        pl.semaphore_signal(barrier, inc=1, device_id=(g, e, o), device_id_type=MESH_ID)
    pl.semaphore_wait(barrier, 6)

    def to_z(k, target, send_index, src=None):
        s = order[k]
        return rcopy(X.at[s, e] if src is None else src, X.at[s, e], z_send.at[send_index], x_recv.at[s, e], (g, e, target))

    def to_x(k, src=None):
        s = order[k]
        return rcopy(X.at[s, e] if src is None else src, X.at[s, e], x_send.at[k], x_recv.at[s, e], (g, e2, z))

    def to_sib(k, src=None):
        s = order[k]
        return rcopy(X.at[s, e] if src is None else src, X.at[s, e], sib_send.at[k], x_recv.at[s, e], (g, e1, z))

    def fwd_sib(k):
        s = order[k]
        return rcopy(X.at[s, e2], X.at[s, e2], fwd_send.at[k], x_recv.at[s, e2], (g, e1, z))

    def arrived(k, b):
        s = order[k]
        rcopy(X.at[s, b], X.at[s, b], x_send.at[k], x_recv.at[s, b], (g, e2, z)).wait_recv()

    turn_s[...] = jnp.zeros_like(turn_s)
    turn_s[:rows, 0:2] = probs[...]
    pt[...] = turn_s[...].T[:8]
    pbuf[e] = pt[...]
    lane = lax.broadcasted_iota(jnp.int32, (all_rows, 128), 1)
    p_copies = [rcopy(pt, pbuf.at[e], p_send.at[i], p_recv.at[e], (g, o, z)) for i, o in enumerate(others_e)]

    to_x(0, tok).start()
    to_z(0, inner, 0, tok).start()

    @pl.when(zz == 1)
    def _():
        to_z(0, outer, 4, tok).start()

    to_sib(0, tok).start()
    for c in p_copies:
        c.start()
    for i in range(4):
        wdload(i).start()
    own = pltpu.make_async_copy(tok, X.at[z, e], local_sem)
    own.start()
    own.wait()

    def forward(k):
        arrived(k, e)

        @pl.when(zz == 1)
        def _():
            to_z(k, inner if k == 1 else outer, k).start()

        to_x(k).start()
        to_sib(k).start()

    requests = req.shape[0]
    per = all_rows // requests
    row = lax.broadcasted_iota(jnp.int32, (all_rows, 128), 0)
    chosen = jnp.zeros((all_rows, 128), jnp.int32)
    for i in range(requests):
        chosen = jnp.where((row >= i * per) & (row < (i + 1) * per), req[i], chosen)
    keep_s[...] = jnp.where(chosen == jnp.where(lane < 64, 0, 1), 1.0, 0.0)
    lat_copies = [
        rcopy(lat_s.at[o], lat_r.at[z], lat_send.at[i], lat_recv.at[z], (g, e, o)) for i, o in enumerate(others_z)
    ]
    sum_copies = [
        rcopy(lat_t.at[z], lat_t.at[z], lt_send.at[i], lt_recv.at[z], (g, e, o)) for i, o in enumerate(others_z)
    ]

    for k in range(4):
        s, slot = order[k], k % 2
        if k == 0:
            forward(1)
        if k < 2:
            @pl.when(zz == 1)
            def _():
                forward(k + 2)

            @pl.when(zz == 0)
            def _():
                if k > 0:
                    forward(k + 1)
        if k == 2:
            @pl.when(zz == 0)
            def _():
                forward(3)
        arrived(k, e2)
        fwd_sib(k).start()
        arrived(k, e1)
        arrived(k, e3)
        if k == 0:
            keep = keep_s[...]
            mixed = jnp.dot(X[s].reshape(all_rows, width), ain[...], preferred_element_type=jnp.float32)
            m0, m1 = mixed[:, :128] * keep, mixed[:, 128:] * keep
            m0 = m0 + pltpu.roll(m0, 64, 1)
            m1 = m1 + pltpu.roll(m1, 64, 1)
            lat_s[...] = jnp.where(lane < 64, m0, m1).astype(jnp.bfloat16).reshape(4, rows, 128)
        if k == 1:
            for c in lat_copies:
                c.start()
        if k == 2:
            for o in others_z:
                rcopy(lat_r.at[o], lat_r.at[o], lat_send.at[0], lat_recv.at[o], (g, e, inner)).wait_recv()
            total = lat_s[z].astype(jnp.float32)
            for o in others_z:
                total = total + lat_r[o].astype(jnp.float32)
            lat_t[z] = total.astype(jnp.bfloat16)
            for c in sum_copies:
                c.start()
            for o in others_e:
                rcopy(pt, pbuf.at[o], p_send.at[0], p_recv.at[o], (g, e2, z)).wait_recv()
            for b in range(4):
                p = pbuf[b].T
                m = jnp.where(routes[b * rows:(b + 1) * rows, :] == e, 1.0, 0.0)
                w = p[:rows, 0:1] * m[:, 0:1] + p[:rows, 1:2] * m[:, 1:2]
                wrow[b // 2, (b % 2) * rows:(b % 2 + 1) * rows, :] = jnp.broadcast_to(w, (rows, 128))
        if k == 3:
            for o in others_z:
                rcopy(lat_t.at[o], lat_t.at[o], lt_send.at[0], lt_recv.at[o], (g, e, inner)).wait_recv()
            total = lat_t[...].reshape(all_rows, 128).astype(jnp.float32)
            keep = keep_s[...]
            turned = pltpu.roll(total, 64, 1)
            spread[0] = (jnp.where(lane < 64, total, turned) * keep).astype(jnp.bfloat16)
            spread[1] = (jnp.where(lane < 64, turned, total) * keep).astype(jnp.bfloat16)
        for c in wload(k):
            c.wait()

        if k < 3:
            @pl.loop(0, hidden // 256)
            def _(j):
                at = pl.ds(pl.multiple_of(j * 256, 256), 256)
                for i in range(2):
                    d = jnp.dot(
                        X[s].reshape(all_rows, width), wbuf[slot, i, :, at], preferred_element_type=jnp.float32
                    )
                    if k == 0:
                        acc[i, :, at] = d
                    else:
                        acc[i, :, at] += d
        else:
            @pl.loop(0, hidden // 256)
            def _(j):
                at = pl.ds(pl.multiple_of(j * 256, 256), 256)
                x = X[s].reshape(all_rows, width)
                v = acc[0, :, at] + jnp.dot(x, wbuf[slot, 0, :, at], preferred_element_type=jnp.float32)
                u = acc[1, :, at] + jnp.dot(x, wbuf[slot, 1, :, at], preferred_element_type=jnp.float32)
                v = v * gs[:, at] + jnp.dot(spread[0], aout[0, :, at], preferred_element_type=jnp.float32)
                u = u * us[:, at] + jnp.dot(spread[1], aout[1, :, at], preferred_element_type=jnp.float32)
                y = (v / (1.0 + jnp.exp(-v)) * u).astype(jnp.bfloat16)
                hid[:, :, at] = y.reshape(2, 2 * rows, 256)
        if k < 2:
            for c in wload(k + 2):
                c.start()

    def s_copy(n, i):
        return rcopy(part.at[n, i, 1 - core], rs_buf.at[n, i], ps_send.at[n, i], ps_recv.at[n, i], (g, e1, z))

    def x_copy(i):
        return rcopy(part.at[0, i, core], rx_buf.at[i], px_send.at[i], px_recv.at[i], (g, e2, z))

    def z_copy(i, middle):
        target, slot = ((inner, 3), (inner, 4), (outer, 3))[i] if middle else (inner, 2 - i)
        return rcopy(part.at[1, i, core], rz_buf.at[slot], pz_send.at[i], pz_recv.at[slot], (g, e, target))

    def z_arrived(slot):
        rcopy(rz_buf.at[slot], rz_buf.at[slot], pz_send.at[0], pz_recv.at[slot], (g, e, inner)).wait_recv()
        return rz_buf[slot].astype(jnp.float32)

    def down(n, i):
        pair = (pair_x, pair_own)[n]
        s = order[3 - i]
        if n == 0:
            wdload(i).wait()

        @pl.loop(0, width // 256)
        def _(j):
            at = pl.ds(pl.multiple_of(j * 256, 256), 256)
            d = jnp.dot(hid[pair], wdb[i, :, at], preferred_element_type=jnp.float32)
            d = d * ds[:, pl.ds(pl.multiple_of(s * width + j * 256, 256), 256)] * wrow[pair, :, 0:1]
            part[n, i, :, :, at] = d.astype(jnp.bfloat16).reshape(2, rows, 256)
        s_copy(n, i).start()

    def send_x(i):
        s_copy(0, i).wait_recv()
        part[0, i, core] = (part[0, i, core].astype(jnp.float32) + rs_buf[0, i].astype(jnp.float32)).astype(
            jnp.bfloat16
        )
        x_copy(i).start()

    def gathered(i):
        s_copy(1, i).wait_recv()
        x_copy(i).wait_recv()
        return (
            part[1, i, core].astype(jnp.float32)
            + rs_buf[1, i].astype(jnp.float32)
            + rx_buf[i].astype(jnp.float32)
        )

    for i in range(4):
        down(0, i)
        if i > 0:
            send_x(i - 1)
    for i in range(4):
        down(1, i)
        if i == 0:
            send_x(3)
    for middle in (False, True):
        @pl.when(zz == int(middle))
        def _():
            for i in range(3):
                total = gathered(i)
                if middle:
                    total = total + z_arrived((2, 1, 3)[i])
                part[1, i, core] = total.astype(jnp.bfloat16)
                z_copy(i, middle).start()
            total = gathered(3)
            for slot in (0, 4) if middle else (3,):
                total = total + z_arrived(slot)
            out[...] = total.astype(jnp.bfloat16)

    to_z(0, inner, 0, tok).wait_send()

    @pl.when(zz == 1)
    def _():
        to_z(0, outer, 4, tok).wait_send()
        for k in (1, 2, 3):
            to_z(k, inner if k == 1 else outer, k).wait_send()

    for k in range(4):
        to_x(k).wait_send()
        to_sib(k).wait_send()
        fwd_sib(k).wait_send()
        x_copy(k).wait_send()
        for n in range(2):
            s_copy(n, k).wait_send()
    for c in p_copies + lat_copies + sum_copies:
        c.wait_send()
    for i in range(3):
        z_copy(i, False).wait_send()


def fused_body(
    tokens, routes, probs, request_adapter, gate_quant_levels, up_quant_levels, down_quant_levels,
    gate_column_scale, up_column_scale, down_column_scale, adapter_input_maps, adapter_output_maps,
):
    rows, width = tokens.shape
    hidden = gate_quant_levels.shape[2]
    all_rows = routes.shape[0]
    vm = pl.BlockSpec(memory_space=pltpu.VMEM)
    hbm = pl.BlockSpec(memory_space=pl.ANY)
    bf, f32 = jnp.bfloat16, jnp.float32
    dma = pltpu.SemaphoreType.DMA
    return pl.pallas_call(
        layer_kernel,
        out_shape=jax.ShapeDtypeStruct((rows, width), bf),
        in_specs=[pl.BlockSpec(memory_space=pltpu.SMEM)] + [vm] * 8 + [hbm] * 3,
        out_specs=vm,
        scratch_shapes=[
            pltpu.VMEM((4, 4, rows, width), bf),
            pltpu.VMEM((2, 2, width, hidden), bf),
            pltpu.VMEM((4, hidden, width), bf),
            pltpu.VMEM((2, all_rows, hidden), f32),
            pltpu.VMEM((2, 2 * rows, hidden), bf),
            pltpu.VMEM((4, rows, 128), bf),
            pltpu.VMEM((4, rows, 128), bf),
            pltpu.VMEM((4, rows, 128), bf),
            pltpu.VMEM((2, all_rows, 128), bf),
            pltpu.VMEM((all_rows, 128), f32),
            pltpu.VMEM((256, 128), f32),
            pltpu.VMEM((8, 256), f32),
            pltpu.VMEM((4, 8, 256), f32),
            pltpu.VMEM((2, 2 * rows, 128), f32),
            pltpu.VMEM((2, 4, 2, rows, width), bf),
            pltpu.VMEM((2, 4, rows, width), bf),
            pltpu.VMEM((4, rows, width), bf),
            pltpu.VMEM((5, rows, width), bf),
            dma, dma((2, 2)), dma((4,)), dma((4, 4)), dma((5,)), dma((4,)), dma((4,)), dma((4,)),
            dma((3,)), dma((4,)), dma((3,)), dma((4,)), dma((3,)), dma((4,)), dma((2, 4)), dma((2, 4)),
            dma((4,)), dma((4,)), dma((3,)), dma((5,)),
        ],
        compiler_params=pltpu.CompilerParams(
            collective_id=0, has_side_effects=True, vmem_limit_bytes=63 * 1024 * 1024
        ),
        cost_estimate=pl.CostEstimate(
            flops=6 * all_rows * 4 * width * hidden, bytes_accessed=6 * 4 * width * hidden, transcendentals=0
        ),
        name="moe_layer",
    )(
        request_adapter, tokens, routes, probs, adapter_input_maps[0], adapter_output_maps[0],
        gate_column_scale, up_column_scale, down_column_scale,
        gate_quant_levels[0], up_quant_levels[0], down_quant_levels[0],
    )


def solution(mesh):
    small = mesh.shape["expert"] == 4 and mesh.shape["tensor"] == 4
    return jax.shard_map(
        fused_body if small else body,
        mesh=mesh,
        in_specs=(
            P(("groups", "expert"), "tensor"),
            P("groups", None),
            P(("groups", "expert"), None),
            P("groups"),
            P("expert", None, "tensor"),
            P("expert", None, "tensor"),
            P("expert", "tensor", None),
            P("expert", "tensor"),
            P("expert", "tensor"),
            P("expert", None),
            P("expert", "tensor", None),
            P("expert", None, None, "tensor"),
        ),
        out_specs=P(("groups", "expert"), "tensor"),
        check_vma=False,
    )
```

```python
import jax
import jax.numpy as jnp
from jax import lax
from jax.experimental import pallas as pl
from jax.experimental.pallas import tpu as pltpu
from jax.sharding import PartitionSpec as P

ADAPTER_RANK = 64
ADAPTER_COUNT = 2


def slot_positions(routes_flat, expert_count):
    experts_range = jnp.arange(expert_count, dtype=jnp.int32)
    onehot = (routes_flat[..., None] == experts_range).astype(jnp.int32)
    earlier = jnp.cumsum(onehot, axis=1) - onehot
    return jnp.sum(onehot * earlier, axis=-1)


def slot_sources(routes_flat, positions, expert_count, capacity, tok_dev):
    blocks = routes_flat.shape[0]
    entries = routes_flat.shape[1]
    experts_range = jnp.arange(expert_count, dtype=jnp.int32)
    slot_range = jnp.arange(capacity, dtype=jnp.int32)
    matched = (
        (routes_flat[None, :, None, :] == experts_range[:, None, None, None])
        & (positions[None, :, None, :] == slot_range[None, None, :, None])
    ).astype(jnp.int32)
    source_row = (
        jnp.arange(blocks, dtype=jnp.int32)[:, None] * tok_dev
        + jnp.arange(entries, dtype=jnp.int32)[None, :] // 2
    )
    found = jnp.sum(matched, axis=-1)
    return jnp.sum(matched * source_row[None, :, None, :], axis=-1) + (1 - found) * (
        blocks * tok_dev
    )


def slot_adapters(routes_flat, positions, entry_adapter, expert_index, capacity):
    slot_range = jnp.arange(capacity, dtype=jnp.int32)
    matched = (
        (routes_flat == expert_index)[:, None, :]
        & (positions[:, None, :] == slot_range[None, :, None])
    ).astype(jnp.float32)
    adapter_hot = (entry_adapter[..., None] == jnp.arange(ADAPTER_COUNT, dtype=jnp.int32)).astype(
        jnp.float32
    )
    return jnp.einsum("bsj,bja->bsa", matched, adapter_hot)


def body(
    tokens,
    routes,
    probs,
    request_adapter,
    gate_quant_levels,
    up_quant_levels,
    down_quant_levels,
    gate_column_scale,
    up_column_scale,
    down_column_scale,
    adapter_input_maps,
    adapter_output_maps,
):
    expert_count = lax.axis_size("expert")
    expert_index = lax.axis_index("expert")
    tok_dev = tokens.shape[0]
    width_part = tokens.shape[1]
    capacity = max(2, min(tok_dev, 3 * (2 * tok_dev // expert_count) // 2))
    slot_count = expert_count * capacity
    requests = request_adapter.shape[0]
    request_length = routes.shape[0] // requests
    routes_flat = routes.reshape(expert_count, 2 * tok_dev)
    positions = slot_positions(routes_flat, expert_count)
    entry_token = (
        jnp.arange(expert_count, dtype=jnp.int32)[:, None] * tok_dev
        + jnp.arange(2 * tok_dev, dtype=jnp.int32)[None, :] // 2
    )
    entry_request = entry_token // request_length
    request_hot = (entry_request[..., None] == jnp.arange(requests, dtype=jnp.int32)).astype(
        jnp.int32
    )
    entry_adapter = jnp.sum(request_hot * request_adapter, axis=-1)
    table = slot_adapters(routes_flat, positions, entry_adapter, expert_index, capacity).reshape(
        -1, ADAPTER_COUNT
    )
    own_routes = lax.dynamic_slice_in_dim(routes_flat, expert_index, 1, 0)[0]
    own_positions = lax.dynamic_slice_in_dim(positions, expert_index, 1, 0)[0]
    sources = slot_sources(
        own_routes[None], own_positions[None], expert_count, capacity, tok_dev
    ).reshape(-1)
    gate_weight = gate_quant_levels[0]
    up_weight = up_quant_levels[0]
    adapter_row_block = adapter_input_maps[0]
    padded = jnp.concatenate([tokens, jnp.zeros((1, width_part), jnp.bfloat16)], axis=0)
    outgoing = jnp.take(padded, sources, axis=0).reshape(expert_count, capacity, width_part)
    arrived = lax.all_to_all(outgoing, "expert", split_axis=0, concat_axis=0, tiled=True).reshape(
        -1, width_part
    )
    piece = lax.all_gather(arrived, "tensor", axis=1, tiled=True)
    gate_next = jnp.dot(piece, gate_weight, preferred_element_type=jnp.float32)
    up_next = jnp.dot(piece, up_weight, preferred_element_type=jnp.float32)
    mixed = jnp.dot(arrived, adapter_row_block, preferred_element_type=jnp.float32)
    gate_plain_term = gate_next * gate_column_scale[0]
    up_plain_term = up_next * up_column_scale[0]
    selected = jnp.sum(
        mixed.reshape(-1, 2, ADAPTER_COUNT, ADAPTER_RANK) * table[:, None, :, None], axis=2
    ).reshape(-1, 2 * ADAPTER_RANK)
    selected = lax.psum(selected, "tensor")
    latent = selected.astype(jnp.bfloat16).reshape(-1, 2, ADAPTER_RANK)
    spread_latent = (latent[:, :, None, :] * table.astype(jnp.bfloat16)[:, None, :, None]).reshape(
        -1, 2, ADAPTER_COUNT * ADAPTER_RANK
    )
    gate_values = gate_plain_term + jnp.dot(
        spread_latent[:, 0], adapter_output_maps[0, 0], preferred_element_type=jnp.float32
    )
    upper_values = up_plain_term + jnp.dot(
        spread_latent[:, 1], adapter_output_maps[0, 1], preferred_element_type=jnp.float32
    )
    hidden = (jax.nn.silu(gate_values) * upper_values).astype(jnp.bfloat16)
    down_weight = down_quant_levels[0]
    down_gain = down_column_scale[0]
    term = lax.dot_general(
        down_weight, hidden, (((0,), (1,)), ((), ())), preferred_element_type=jnp.float32
    )
    summed = lax.psum_scatter(
        (term * down_gain[:, None]).astype(jnp.bfloat16), "tensor", scatter_dimension=0, tiled=True
    )
    returned = lax.all_to_all(
        summed.reshape(width_part, expert_count, capacity),
        "expert",
        split_axis=1,
        concat_axis=1,
        tiled=True,
    ).reshape(width_part, slot_count)
    targets = own_routes * capacity + own_positions
    match = (
        (jnp.arange(slot_count, dtype=jnp.int32)[:, None] == targets[None, :])
        .astype(jnp.float32)
        .reshape(slot_count, tok_dev, 2)
    )
    combine = jnp.sum(match * probs[None, :, :], axis=2)
    output = lax.dot_general(
        combine,
        returned.astype(jnp.float32),
        (((0,), (1,)), ((), ())),
        precision=lax.Precision.HIGHEST,
        preferred_element_type=jnp.float32,
    )
    return output.astype(jnp.bfloat16)


MESH_ID = pl.DeviceIdType.MESH


def rcopy(src, dst, send, recv, device):
    return pltpu.make_async_remote_copy(
        src_ref=src, dst_ref=dst, send_sem=send, recv_sem=recv, device_id=device, device_id_type=MESH_ID
    )


def layer_kernel(
    req, tok, routes, probs, ain, aout, gs, us, ds, wg, wu, wd, out,
    X, wbuf, wdb, acc, hid, lat_s, lat_r, lat_t, spread, keep_s, turn_s, pt, pbuf, wrow, part, rs_buf, rx_buf, rz_buf,
    local_sem, w_sem, wd_sem, x_recv, z_send, x_send, sib_send, fwd_send,
    p_send, p_recv, lat_send, lat_recv, lt_send, lt_recv, ps_send, ps_recv, px_send, px_recv, pz_send, pz_recv,
):
    rows, width = tok.shape
    hidden = wbuf.shape[3]
    all_rows = 4 * rows
    g, e, z = lax.axis_index("groups"), lax.axis_index("expert"), lax.axis_index("tensor")
    core = e % 2
    e1 = e + 1 - 2 * core
    e2 = (e + 2) % 4
    e3 = (e1 + 2) % 4
    pair_x, pair_own = 1 - e // 2, e // 2
    h = z // 2
    zz = z * (1 - h) + (3 - z) * h
    order = [b * (1 - h) + (3 - b) * h for b in (zz, 1 - zz, 2, 3)]
    inner = z + 1 - 2 * h
    outer = (z - 1 + 2 * h + 4) % 4
    others_e = (e1, e2, e3)
    others_z = tuple((z + d) % 4 for d in (1, 2, 3))

    def wload(k):
        s, slot = order[k], k % 2
        at = pl.ds(pl.multiple_of(s * width, width), width)
        return [
            pltpu.make_async_copy(w.at[at, :], wbuf.at[slot, i], w_sem.at[slot, i])
            for i, w in enumerate((wg, wu))
        ]

    def wdload(i):
        s = order[3 - i]
        return pltpu.make_async_copy(
            wd.at[:, pl.ds(pl.multiple_of(s * width, width), width)], wdb.at[i], wd_sem.at[i]
        )

    for k in (0, 1):
        for c in wload(k):
            c.start()
    barrier = pltpu.get_barrier_semaphore()
    for o in others_e:
        pl.semaphore_signal(barrier, inc=1, device_id=(g, o, z), device_id_type=MESH_ID)
    for o in others_z:
        pl.semaphore_signal(barrier, inc=1, device_id=(g, e, o), device_id_type=MESH_ID)
    pl.semaphore_wait(barrier, 6)

    def to_z(k, target, send_index, src=None):
        s = order[k]
        return rcopy(X.at[s, e] if src is None else src, X.at[s, e], z_send.at[send_index], x_recv.at[s, e], (g, e, target))

    def to_x(k, src=None):
        s = order[k]
        return rcopy(X.at[s, e] if src is None else src, X.at[s, e], x_send.at[k], x_recv.at[s, e], (g, e2, z))

    def to_sib(k, src=None):
        s = order[k]
        return rcopy(X.at[s, e] if src is None else src, X.at[s, e], sib_send.at[k], x_recv.at[s, e], (g, e1, z))

    def fwd_sib(k):
        s = order[k]
        return rcopy(X.at[s, e2], X.at[s, e2], fwd_send.at[k], x_recv.at[s, e2], (g, e1, z))

    def arrived(k, b):
        s = order[k]
        rcopy(X.at[s, b], X.at[s, b], x_send.at[k], x_recv.at[s, b], (g, e2, z)).wait_recv()

    turn_s[...] = jnp.zeros_like(turn_s)
    pt[...] = jnp.zeros_like(pt)
    pt[0:2, 0:rows] = probs[...]
    pbuf[e] = pt[...]
    lane = lax.broadcasted_iota(jnp.int32, (all_rows, 128), 1)
    p_copies = [rcopy(pt, pbuf.at[e], p_send.at[i], p_recv.at[e], (g, o, z)) for i, o in enumerate(others_e)]

    to_x(0, tok).start()
    to_z(0, inner, 0, tok).start()

    @pl.when(zz == 1)
    def _():
        to_z(0, outer, 4, tok).start()

    to_sib(0, tok).start()
    for c in p_copies:
        c.start()
    for i in range(4):
        wdload(i).start()
    own = pltpu.make_async_copy(tok, X.at[z, e], local_sem)
    own.start()
    own.wait()

    def forward(k):
        arrived(k, e)

        @pl.when(zz == 1)
        def _():
            to_z(k, inner if k == 1 else outer, k).start()

        to_x(k).start()
        to_sib(k).start()

    requests = req.shape[0]
    per = all_rows // requests
    row = lax.broadcasted_iota(jnp.int32, (all_rows, 128), 0)
    chosen = jnp.zeros((all_rows, 128), jnp.int32)
    for i in range(requests):
        chosen = jnp.where((row >= i * per) & (row < (i + 1) * per), req[i], chosen)
    keep_s[...] = jnp.where(chosen == jnp.where(lane < 64, 0, 1), 1.0, 0.0)
    lat_copies = [
        rcopy(lat_s.at[o], lat_r.at[z], lat_send.at[i], lat_recv.at[z], (g, e, o)) for i, o in enumerate(others_z)
    ]
    sum_copies = [
        rcopy(lat_t.at[z], lat_t.at[z], lt_send.at[i], lt_recv.at[z], (g, e, o)) for i, o in enumerate(others_z)
    ]

    for k in range(4):
        s, slot = order[k], k % 2
        if k == 0:
            forward(1)
        if k < 2:
            @pl.when(zz == 1)
            def _():
                forward(k + 2)

            @pl.when(zz == 0)
            def _():
                if k > 0:
                    forward(k + 1)
        if k == 2:
            @pl.when(zz == 0)
            def _():
                forward(3)
        arrived(k, e2)
        fwd_sib(k).start()
        arrived(k, e1)
        arrived(k, e3)
        if k == 0:
            keep = keep_s[...]
            mixed = jnp.dot(X[s].reshape(all_rows, width), ain[...], preferred_element_type=jnp.float32)
            m0, m1 = mixed[:, :128] * keep, mixed[:, 128:] * keep
            m0 = m0 + pltpu.roll(m0, 64, 1)
            m1 = m1 + pltpu.roll(m1, 64, 1)
            lat_s[...] = jnp.where(lane < 64, m0, m1).astype(jnp.bfloat16).reshape(4, rows, 128)
        if k == 1:
            for c in lat_copies:
                c.start()
        if k == 2:
            for o in others_z:
                rcopy(lat_r.at[o], lat_r.at[o], lat_send.at[0], lat_recv.at[o], (g, e, inner)).wait_recv()
            total = lat_s[z].astype(jnp.float32)
            for o in others_z:
                total = total + lat_r[o].astype(jnp.float32)
            lat_t[z] = total.astype(jnp.bfloat16)
            for c in sum_copies:
                c.start()
            for o in others_e:
                rcopy(pt, pbuf.at[o], p_send.at[0], p_recv.at[o], (g, e2, z)).wait_recv()
            for b in range(4):
                m = jnp.where(routes[:, b * rows:(b + 1) * rows] == e, 1.0, 0.0)
                turn_s[0:2, 0:rows] = pbuf[b, 0:2, 0:rows] * m
                w = turn_s[...].T
                w = w[:rows, 0:1] + w[:rows, 1:2]
                wrow[b // 2, (b % 2) * rows:(b % 2 + 1) * rows, :] = jnp.broadcast_to(w, (rows, 128))
        if k == 3:
            for o in others_z:
                rcopy(lat_t.at[o], lat_t.at[o], lt_send.at[0], lt_recv.at[o], (g, e, inner)).wait_recv()
            total = lat_t[...].reshape(all_rows, 128).astype(jnp.float32)
            keep = keep_s[...]
            turned = pltpu.roll(total, 64, 1)
            spread[0] = (jnp.where(lane < 64, total, turned) * keep).astype(jnp.bfloat16).reshape(2, 2 * rows, 128)
            spread[1] = (jnp.where(lane < 64, turned, total) * keep).astype(jnp.bfloat16).reshape(2, 2 * rows, 128)
        for c in wload(k):
            c.wait()

        if k < 3:
            @pl.loop(0, hidden // 512)
            def _(j):
                at = pl.ds(pl.multiple_of(j * 512, 512), 512)
                for i in range(2):
                    d = jnp.dot(
                        X[s].reshape(all_rows, width), wbuf[slot, i, :, at], preferred_element_type=jnp.float32
                    )
                    d = d.reshape(2, 2 * rows, 512)
                    if k == 0:
                        acc[i, :, :, at] = d
                    else:
                        acc[i, :, :, at] += d
        if k < 2:
            for c in wload(k + 2):
                c.start()

    def s_copy(n, i):
        return rcopy(part.at[n, i, 1 - core], rs_buf.at[n, i], ps_send.at[n, i], ps_recv.at[n, i], (g, e1, z))

    def x_copy(i):
        return rcopy(part.at[0, i, core], rx_buf.at[i], px_send.at[i], px_recv.at[i], (g, e2, z))

    def z_copy(i, middle):
        target, slot = ((inner, 3), (inner, 4), (outer, 3))[i] if middle else (inner, 2 - i)
        return rcopy(part.at[1, i, core], rz_buf.at[slot], pz_send.at[i], pz_recv.at[slot], (g, e, target))

    def z_arrived(slot):
        rcopy(rz_buf.at[slot], rz_buf.at[slot], pz_send.at[0], pz_recv.at[slot], (g, e, inner)).wait_recv()
        return rz_buf[slot].astype(jnp.float32)

    def down(n, i):
        pair = (pair_x, pair_own)[n]
        s = order[3 - i]
        if n == 0:
            wdload(i).wait()

        @pl.loop(0, width // 768)
        def _(j):
            at = pl.ds(pl.multiple_of(j * 768, 768), 768)
            d = jnp.dot(hid[pair], wdb[i, :, at], preferred_element_type=jnp.float32)
            d = d * ds[:, pl.ds(pl.multiple_of(s * width + j * 768, 768), 768)] * wrow[pair, :, 0:1]
            part[n, i, :, :, at] = d.astype(jnp.bfloat16).reshape(2, rows, 768)
        s_copy(n, i).start()

    def send_x(i):
        s_copy(0, i).wait_recv()
        part[0, i, core] = (part[0, i, core].astype(jnp.float32) + rs_buf[0, i].astype(jnp.float32)).astype(
            jnp.bfloat16
        )
        x_copy(i).start()

    def gathered(i):
        s_copy(1, i).wait_recv()
        x_copy(i).wait_recv()
        return (
            part[1, i, core].astype(jnp.float32)
            + rs_buf[1, i].astype(jnp.float32)
            + rx_buf[i].astype(jnp.float32)
        )

    def finish(pair):
        s, slot = order[3], 1

        @pl.loop(0, hidden // 512)
        def _(j):
            at = pl.ds(pl.multiple_of(j * 512, 512), 512)
            x = X[s, pl.ds(pair * 2, 2)].reshape(2 * rows, width)
            v = acc[0, pair, :, at] + jnp.dot(x, wbuf[slot, 0, :, at], preferred_element_type=jnp.float32)
            u = acc[1, pair, :, at] + jnp.dot(x, wbuf[slot, 1, :, at], preferred_element_type=jnp.float32)
            v = v * gs[:, at] + jnp.dot(spread[0, pair], aout[0, :, at], preferred_element_type=jnp.float32)
            u = u * us[:, at] + jnp.dot(spread[1, pair], aout[1, :, at], preferred_element_type=jnp.float32)
            hid[pair, :, at] = (v / (1.0 + jnp.exp(-v)) * u).astype(jnp.bfloat16)

    finish(pair_x)
    for i in range(4):
        down(0, i)
        if i > 0:
            send_x(i - 1)
    send_x(3)
    finish(pair_own)
    for i in range(4):
        down(1, i)
    for middle in (False, True):
        @pl.when(zz == int(middle))
        def _():
            for i in range(3):
                total = gathered(i)
                if middle:
                    total = total + z_arrived((2, 1, 3)[i])
                part[1, i, core] = total.astype(jnp.bfloat16)
                z_copy(i, middle).start()
            total = gathered(3)
            for slot in (0, 4) if middle else (3,):
                total = total + z_arrived(slot)
            out[...] = total.astype(jnp.bfloat16)

    to_z(0, inner, 0, tok).wait_send()

    @pl.when(zz == 1)
    def _():
        to_z(0, outer, 4, tok).wait_send()
        for k in (1, 2, 3):
            to_z(k, inner if k == 1 else outer, k).wait_send()

    for k in range(4):
        to_x(k).wait_send()
        to_sib(k).wait_send()
        fwd_sib(k).wait_send()
        x_copy(k).wait_send()
        for n in range(2):
            s_copy(n, k).wait_send()
    for c in p_copies + lat_copies + sum_copies:
        c.wait_send()
    for i in range(3):
        z_copy(i, False).wait_send()


def fused_body(
    tokens, routes, probs, request_adapter, gate_quant_levels, up_quant_levels, down_quant_levels,
    gate_column_scale, up_column_scale, down_column_scale, adapter_input_maps, adapter_output_maps,
):
    rows, width = tokens.shape
    hidden = gate_quant_levels.shape[2]
    all_rows = routes.shape[0]
    vm = pl.BlockSpec(memory_space=pltpu.VMEM)
    hbm = pl.BlockSpec(memory_space=pl.ANY)
    bf, f32 = jnp.bfloat16, jnp.float32
    dma = pltpu.SemaphoreType.DMA
    return pl.pallas_call(
        layer_kernel,
        out_shape=jax.ShapeDtypeStruct((rows, width), bf),
        in_specs=[pl.BlockSpec(memory_space=pltpu.SMEM)] + [vm] * 8 + [hbm] * 3,
        out_specs=vm,
        scratch_shapes=[
            pltpu.VMEM((4, 4, rows, width), bf),
            pltpu.VMEM((2, 2, width, hidden), bf),
            pltpu.VMEM((4, hidden, width), bf),
            pltpu.VMEM((2, 2, 2 * rows, hidden), f32),
            pltpu.VMEM((2, 2 * rows, hidden), bf),
            pltpu.VMEM((4, rows, 128), bf),
            pltpu.VMEM((4, rows, 128), bf),
            pltpu.VMEM((4, rows, 128), bf),
            pltpu.VMEM((2, 2, 2 * rows, 128), bf),
            pltpu.VMEM((all_rows, 128), f32),
            pltpu.VMEM((8, 256), f32),
            pltpu.VMEM((8, 256), f32),
            pltpu.VMEM((4, 8, 256), f32),
            pltpu.VMEM((2, 2 * rows, 128), f32),
            pltpu.VMEM((2, 4, 2, rows, width), bf),
            pltpu.VMEM((2, 4, rows, width), bf),
            pltpu.VMEM((4, rows, width), bf),
            pltpu.VMEM((5, rows, width), bf),
            dma, dma((2, 2)), dma((4,)), dma((4, 4)), dma((5,)), dma((4,)), dma((4,)), dma((4,)),
            dma((3,)), dma((4,)), dma((3,)), dma((4,)), dma((3,)), dma((4,)), dma((2, 4)), dma((2, 4)),
            dma((4,)), dma((4,)), dma((3,)), dma((5,)),
        ],
        compiler_params=pltpu.CompilerParams(
            collective_id=0, has_side_effects=True, vmem_limit_bytes=63 * 1024 * 1024
        ),
        cost_estimate=pl.CostEstimate(
            flops=6 * all_rows * 4 * width * hidden, bytes_accessed=6 * 4 * width * hidden, transcendentals=0
        ),
        name="moe_layer",
    )(
        request_adapter, tokens, routes.T, probs.T, adapter_input_maps[0], adapter_output_maps[0],
        gate_column_scale, up_column_scale, down_column_scale,
        gate_quant_levels[0], up_quant_levels[0], down_quant_levels[0],
    )


def solution(mesh):
    small = mesh.shape["expert"] == 4 and mesh.shape["tensor"] == 4
    return jax.shard_map(
        fused_body if small else body,
        mesh=mesh,
        in_specs=(
            P(("groups", "expert"), "tensor"),
            P("groups", None),
            P(("groups", "expert"), None),
            P("groups"),
            P("expert", None, "tensor"),
            P("expert", None, "tensor"),
            P("expert", "tensor", None),
            P("expert", "tensor"),
            P("expert", "tensor"),
            P("expert", None),
            P("expert", "tensor", None),
            P("expert", None, None, "tensor"),
        ),
        out_specs=P(("groups", "expert"), "tensor"),
        check_vma=False,
    )
```
